256 devices in a mesh: sub: 16 (over y, x_lo, core), grp: 16 (over z, x_hi).
Axes of the slice: x: 4 (x_hi: 2, x_lo: 2; x = x_hi * 2 + x_lo), y: 4, z: 8, core: 2. Of those that a mesh axis runs over, the one named last changes fastest.
Arguments:
- child_fronts: float32 [16, 4096, 4096], P('sub', 'grp'), as said below
- child_pattern: int32 [16, 16, 16], P('sub'), may hold values from 0 to 1, as said below
- child_maps: int32 [16, 15], P('sub'), may hold values from 0 to 15, as said below
- parent_fronts: float32 [16, 4096, 2048], P('sub', 'grp'), as said below
Outputs:
- child_panels: float32 [16, 4096, 256], P('sub', 'grp')
- parent_result: float32 [16, 4096, 2048], P('sub', 'grp')
The draws below stay inside these ranges and needn't reach their ends.
Inputs may be any that keep to these rules, and one draw needn't show every extreme that they name: `child_fronts`: each child front is symmetric positive definite. `parent_fronts`: each parent front's initial entries, put together from the column blocks at indices 2p and 2p + 1 as in the reference program, form a symmetric positive definite matrix. `child_pattern`: each child's pattern is symmetric with ones on its diagonal. `child_maps`: each row is strictly increasing and ends with 15.
All inputs are finite; a program needn't handle non-finite values.
Results may differ from the reference program's by a relative error of at most 0.0003.
Values sent between devices are 32-bit elements; how exact they have to be, the bound alone decides.
No kernel may reach another device: no remote copies, remote signals or barrier semaphores. Data moves between devices by JAX's collectives and lax.ppermute only.
A program may use at most 128 MiB of HBM per device.

```python
import math
import jax
import jax.numpy as jnp
from jax import lax

TILE = 256
FRONT = 4096
PIV1 = 1
PIV2 = 2
NB = 16
UB = 15
N_SUB = 16


def block_coupling(key):
    ranks = 8
    factors = jax.random.normal(key, (NB, TILE, ranks), jnp.float32) * (1.0 / math.sqrt(TILE))
    coupled = jnp.zeros((NB, TILE, TILE), jnp.float32)
    for rank_index in range(ranks):
        column = factors[:, :, rank_index]
        coupled = coupled + column[:, :, None] * column[:, None, :]
    same_block = jnp.eye(NB, dtype=jnp.float32) > 0.5
    placed = jnp.where(same_block[:, None, :, None], coupled[:, :, None, :], 0.0)
    return placed.reshape(FRONT, FRONT)


def symmetric_front(key):
    first_key = jax.random.fold_in(key, 11)
    second_key = jax.random.fold_in(key, 12)
    fourth_key = jax.random.fold_in(key, 14)
    noise = jax.random.normal(first_key, (FRONT, FRONT), jnp.float32)
    scale = 1.0 / (4.0 * math.sqrt(FRONT))
    symmetric = (noise + noise.T) * (0.7071 * scale)
    diagonal = jax.random.uniform(second_key, (FRONT,), jnp.float32, 0.75, 1.5)
    matrix = symmetric + jnp.diag(diagonal) + block_coupling(fourth_key)
    return matrix


def draw_child_fronts(key, part):
    keys = jax.random.split(jax.random.fold_in(key, 101), N_SUB)
    return jax.lax.map(symmetric_front, keys)


def draw_parent_fronts(key, part):
    keys = jax.random.split(jax.random.fold_in(key, 202), N_SUB // 2)
    fronts = jax.lax.map(symmetric_front, keys)
    blocked = fronts.reshape(N_SUB // 2, FRONT, NB // 2, 2, TILE)
    return jnp.transpose(blocked, (0, 3, 1, 2, 4)).reshape(N_SUB, FRONT, FRONT // 2)


def draw_child_pattern(key, part):
    bits = jax.random.randint(jax.random.fold_in(key, 303), (N_SUB, NB, NB), 0, 2)
    indices = jnp.arange(NB)
    upper = jnp.where((indices[:, None] <= indices[None, :])[None], bits, jnp.swapaxes(bits, 1, 2))
    return jnp.where((indices[:, None] == indices[None, :])[None], 1, upper).astype(jnp.int32)


def draw_child_maps(key, part):
    keys = jax.random.split(jax.random.fold_in(key, 404), N_SUB)

    def one_map(single):
        shuffled = jax.random.permutation(single, NB - 1)
        picked = jnp.sort(shuffled[:UB - 1])
        return jnp.concatenate([picked, jnp.full((1,), NB - 1, jnp.int32)]).astype(jnp.int32)
    return jax.vmap(one_map)(keys)


def setup_inputs(seed: int = 0) -> dict:
    arg_keys = jax.random.split(jax.random.key(seed), 5)
    return {
        "child_fronts": draw_child_fronts(jax.random.fold_in(arg_keys[4], 71), 0),
        "child_pattern": draw_child_pattern(jax.random.fold_in(arg_keys[4], 71), 0),
        "child_maps": draw_child_maps(jax.random.fold_in(arg_keys[4], 71), 0),
        "parent_fronts": draw_parent_fronts(jax.random.fold_in(arg_keys[4], 71), 0),
    }


precise = lax.Precision.HIGHEST

def eliminate(matrix, pivots):
    extent = matrix.shape[0]
    blocks = jnp.arange(extent) // TILE
    columns = []
    for pivot_index in range(pivots):
        offset = pivot_index * TILE
        factor = jnp.linalg.cholesky(matrix[offset:offset + TILE, offset:offset + TILE])
        solved = lax.linalg.triangular_solve(factor, matrix[:, offset:offset + TILE], left_side=False, lower=True, transpose_a=True)
        below = jnp.where((blocks > pivot_index)[:, None], solved, 0.0)
        matrix = matrix - jnp.dot(below, below.T, precision=precise)
        diagonal_rows = jnp.tile(factor, (extent // TILE, 1))
        columns.append(jnp.where((blocks == pivot_index)[:, None], diagonal_rows, below))
    panel_cols = jnp.concatenate(columns, axis=1)
    result = jnp.where((blocks < pivots)[:, None], 0.0, matrix)
    result = result.at[:, :pivots * TILE].set(panel_cols)
    return (result, panel_cols)

def child_front(front, pattern, mapping):
    block_mask = jnp.repeat(jnp.repeat(pattern, TILE, axis=0), TILE, axis=1)
    masked = jnp.where(block_mask > 0, front, 0.0)
    result, panel_cols = eliminate(masked, PIV1)
    update = result[PIV1 * TILE:, PIV1 * TILE:]
    placed = (mapping[:, None] * TILE + jnp.arange(TILE, dtype=jnp.int32)[None, :]).reshape(-1).astype(jnp.int32)
    spread = jnp.zeros((FRONT, FRONT), jnp.float32).at[placed[:, None], placed[None, :]].set(update.T)
    return (panel_cols, spread)

def reference(child_fronts, child_pattern, child_maps, parent_fronts):
    half_cols = FRONT // 2
    parents = N_SUB // 2
    half_blocks = NB // 2

    def one_parent(members):
        fronts, patterns, mappings, initial = members
        panel_first, spread_first = child_front(fronts[0], patterns[0], mappings[0])
        panel_second, spread_second = child_front(fronts[1], patterns[1], mappings[1])
        first = initial[0].reshape(FRONT, half_blocks, TILE)
        second = initial[1].reshape(FRONT, half_blocks, TILE)
        joined = jnp.stack([first, second], axis=2).reshape(FRONT, FRONT)
        parent = joined + spread_first + spread_second
        result, unused = eliminate(parent, PIV2)
        split = result.reshape(FRONT, half_blocks, 2, TILE)
        packed = jnp.stack([split[:, :, 0, :].reshape(FRONT, half_cols), split[:, :, 1, :].reshape(FRONT, half_cols)])
        return (jnp.stack([panel_first, panel_second]), packed)
    panels, packed = lax.map(one_parent, (child_fronts.reshape(parents, 2, FRONT, FRONT), child_pattern.reshape(parents, 2, NB, NB), child_maps.reshape(parents, 2, UB), parent_fronts.reshape(parents, 2, FRONT, half_cols)))
    return (panels.reshape(N_SUB, FRONT, PIV1 * TILE), packed.reshape(N_SUB, FRONT, half_cols))
```

```python
import jax
import jax.numpy as jnp
from jax import lax
from jax.sharding import PartitionSpec as P

TILE = 256
HIGH = lax.Precision.HIGH
BEST = lax.Precision.HIGHEST


def mm(a, b, precision=HIGH):
    return jnp.dot(a, b, precision=precision)


def mt(a, b, precision=HIGH):
    return lax.dot_general(a, b, (((1,), (1,)), ((), ())), precision=precision)


def tied(value, *after):
    return lax.optimization_barrier((value, *after))[0]


def at(z, x):
    return (z % 8) * 2 + x % 2


def send_grp(block, pairs):
    return lax.ppermute(block, "grp", pairs)


def swap_core(block):
    return lax.ppermute(block, "sub", [(i, i ^ 1) for i in range(16)])


def broadcast(block, root, me):
    z0, x0 = root // 2, root % 2

    def rel(z, x):
        return at(z0 + z, x0 + x)

    mine = jnp.where(me == root, block, 0.0)
    first = [send_grp(block, [(root, rel(z, x))]) for z, x in ((2, 0), (6, 0), (0, 1), (4, 0))]
    held = mine + first[0] + first[1] + first[2] + first[3]
    rounds = (
        [((0, 0), (1, 0)), ((2, 0), (3, 0)), ((6, 0), (5, 0)), ((4, 0), (4, 1)), ((0, 1), (1, 1))],
        [((0, 0), (7, 0)), ((2, 0), (2, 1)), ((6, 0), (6, 1)), ((0, 1), (7, 1)), ((4, 0), (3, 1))],
        [((4, 0), (5, 1))],
    )
    second = [send_grp(held, [(rel(*s), rel(*t)) for s, t in pairs]) for pairs in rounds]
    return held + second[0] + second[1] + second[2]


def ring_z(block, z):
    rows = block.shape[0]
    up_pairs = [(i, (i + 2) % 16) for i in range(16)]
    down_pairs = [(i, (i - 2) % 16) for i in range(16)]
    whole = jnp.zeros((8 * rows, block.shape[1]), block.dtype)

    def put(whole, piece, place):
        return lax.dynamic_update_slice_in_dim(whole, piece, (place % 8) * rows, 0)

    whole = put(whole, block, z)
    up = down = block
    for step in range(1, 4):
        up, down = send_grp(up, up_pairs), send_grp(down, down_pairs)
        whole = put(whole, up, z - step + 8)
        whole = put(whole, down, z + step)
    half = rows // 2
    last = jnp.concatenate(
        [send_grp(up[:half], up_pairs), send_grp(down[half:], down_pairs)], axis=0
    )
    return put(whole, last, z + 4)


def factor(block):
    lower = jnp.linalg.cholesky(block)
    inverse = lax.linalg.triangular_solve(
        lower, jnp.eye(TILE, dtype=block.dtype), left_side=True, lower=True
    )
    return lower, inverse


def on_device(child_fronts, child_pattern, child_maps, parent_fronts):
    raw = child_fronts[0]
    height, extent = raw.shape
    nblocks = extent // TILE
    me = lax.axis_index("grp")
    core = lax.axis_index("sub") % 2
    z, x = me // 2, me % 2
    pattern = child_pattern[0]
    mapping = child_maps[0]
    front = parent_fronts[0]
    blocks = jnp.arange(nblocks)
    miss = jnp.sum((mapping == jnp.arange(nblocks - 1)).astype(jnp.int32))

    def masked(strip, row, first, count):
        kept = lax.dynamic_index_in_dim(pattern, jnp.minimum(row, nblocks - 1), 0, keepdims=False)
        kept = jnp.repeat(kept[first : first + count], TILE, total_repeat_length=count * TILE)
        return jnp.where((kept > 0)[None, :], strip, 0.0)

    first_own = masked(raw[:, :TILE], me, 0, 1)
    diagonal = broadcast(first_own, 0, me)
    shift = [((i + 1) % 16, i) for i in range(16)]
    head_next = send_grp(tied(raw[:, : 3 * TILE], diagonal), shift)
    column_1 = broadcast(tied(first_own, diagonal), 1, me)
    column_2 = broadcast(tied(first_own, diagonal), 2, me)

    partner = send_grp(tied(first_own, column_1, column_2), [(i, i ^ 1) for i in range(16)])
    pair = jnp.where(
        x == 0,
        jnp.concatenate([first_own, partner], axis=0),
        jnp.concatenate([partner, first_own], axis=0),
    )
    column = ring_z(pair, z)
    tail_next = send_grp(tied(raw[:, 3 * TILE :], head_next), shift)

    lower, inverse = factor(diagonal)
    below_own = mt(first_own, inverse)
    child_panels = jnp.where(me == 0, lower, below_own)[None]

    def chosen(own, following, first, count):
        own = masked(own, me, first, count)
        following = masked(following, me + 1, first, count)
        return jnp.where(me < miss, following, jnp.where(me > miss, own, 0.0))

    head = chosen(raw[:, : 3 * TILE], head_next, 0, 3)
    weight = mm(mt(head[:, :TILE], inverse), inverse)
    update_1 = head[:, TILE : 2 * TILE] - mt(weight, column_1)
    update_2 = head[:, 2 * TILE :] - mt(weight, column_2)
    pivot_0 = jnp.where(miss > 0, update_1, 0.0)
    pivot_1 = jnp.where(miss > 1, update_2, jnp.where(miss < 1, update_1, 0.0))
    pivots = jnp.concatenate([pivot_0, pivot_1], axis=1)
    pivots = pivots + jnp.concatenate(
        [
            jnp.where(core == 0, front[:, :TILE], 0.0),
            jnp.where(core == 1, front[:, :TILE], 0.0),
        ],
        axis=1,
    )
    pivots = pivots + swap_core(pivots)

    corner_0 = broadcast(pivots[:, :TILE], 0, me)
    own_part = jnp.where(core == 0, pivots[:, :TILE], pivots[:, TILE:])
    row_1 = broadcast(tied(own_part, corner_0), 1, me)
    row_1_other = swap_core(row_1)
    corner_10 = jnp.where(core == 0, row_1, row_1_other)
    corner_11 = jnp.where(core == 0, row_1_other, row_1)

    pairs = []
    for sub in range(16):
        for place in range(8):
            source, target = place * 2 + sub % 2, place * 2 + 1 - sub % 2
            pairs.append((sub * 16 + source, sub * 16 + target))
    across = lax.ppermute(tied(pivots, corner_0), ("sub", "grp"), pairs)
    pivot_rows = ring_z(jnp.where(x == core, pivots, across), z)

    strip = jnp.concatenate([head, chosen(raw[:, 3 * TILE :], tail_next, 3, nblocks - 3)], axis=1)
    update = strip - mt(weight, column)
    place = jnp.repeat(jnp.arange(2, nblocks), TILE, total_repeat_length=extent - 2 * TILE)[None, :]
    later = jnp.concatenate([update[:, 3 * TILE :], update[:, :TILE]], axis=1)
    spread = jnp.where(place < miss, later, jnp.where(place > miss, update[:, 2 * TILE :], 0.0))
    paired = spread.reshape(height, nblocks // 2 - 1, 2, TILE)
    even = paired[:, :, 0].reshape(height, -1)
    odd = paired[:, :, 1].reshape(height, -1)
    theirs = swap_core(jnp.where(core == 0, odd, even))
    base = front[:, TILE:] + (jnp.where(core == 0, even, odd) + theirs)

    lower_0, inverse_0 = factor(corner_0)
    below_10 = mt(corner_10, inverse_0)
    lower_1, inverse_1 = factor(corner_11 - mt(below_10, below_10))
    below_0 = mt(pivots[:, :TILE], inverse_0)
    below_1 = mt(pivots[:, TILE:] - mt(below_0, below_10), inverse_1)
    weight_1 = mm(below_1, inverse_1)
    weight_0 = mm(below_0 - mm(weight_1, below_10), inverse_0)
    weights = jnp.concatenate([weight_0, weight_1], axis=1)
    schur = base - mt(weights, pivot_rows[TILE:])
    schur = jnp.where(me < 2, 0.0, schur)
    panel_0 = jnp.where(me == 0, lower_0, below_0)
    panel_1 = jnp.where(me == 0, 0.0, jnp.where(me == 1, lower_1, below_1))
    panel = jnp.where(core == 0, panel_0, panel_1)
    result = jnp.concatenate([panel, schur], axis=1)
    return (child_panels, result[None])


def solution(mesh):
    in_specs = (P("sub", "grp", None), P("sub", None, None), P("sub", None), P("sub", "grp", None))
    out_specs = (P("sub", "grp", None), P("sub", "grp", None))
    return jax.shard_map(
        on_device, mesh=mesh, in_specs=in_specs, out_specs=out_specs, check_vma=False
    )
```

```python
import jax
import jax.numpy as jnp
from jax import lax
from jax.experimental import pallas as pl
from jax.experimental.pallas import tpu as pltpu
from jax.sharding import PartitionSpec as P

TILE = 256
STEP = 64
NN, NT, TN = ((1,), (0,)), ((1,), (1,)), ((0,), (0,))
F32 = jnp.float32
SMEM = pl.BlockSpec(memory_space=pltpu.SMEM)
VMEM = pl.BlockSpec(memory_space=pltpu.VMEM)


def product(a, b, dims):
    return lax.dot_general(
        a, b, (dims, ((), ())), precision=lax.Precision.HIGHEST, preferred_element_type=F32
    )


def cost(us, moved):
    return pl.CostEstimate(flops=int(us * 1e9), bytes_accessed=moved, transcendentals=0)


def small_block(tile, base, sub):
    rows = [tile[8 * q : 8 * q + 8, :] for q in range(8)]
    done = []
    for p in range(8):
        lanes = [base + 8 * p + l for l in range(8)]
        def column(q, l):
            return jnp.broadcast_to(rows[q][:, lanes[l] : lanes[l] + 1], (8, 128))
        own = [column(p, l) for l in range(8)]
        s = [[None] * 8 for _ in range(8)]
        for i in range(8):
            for l in range(i + 1):
                s[i][l] = jnp.broadcast_to(own[l][i : i + 1, :], (8, 128))
        later = {q: [column(q, l) for l in range(8)] for q in range(p + 1, 8)}
        m = [[None] * 8 for _ in range(8)]
        inv = []
        for j in range(8):
            r = 1.0 / s[j][j]
            inv.append(r)
            for i in range(j + 1, 8):
                m[i][j] = s[i][j] * r
            for i in range(j + 1, 8):
                for k in range(j + 1, i + 1):
                    s[i][k] = s[i][k] - m[i][j] * s[k][j]
        n = [[None] * 8 for _ in range(8)]
        for j in range(8):
            for i in range(j + 1, 8):
                total = m[i][j]
                for k in range(j + 1, i):
                    total = total + m[i][k] * n[k][j]
                n[i][j] = -total
        rowb = [jnp.broadcast_to(rows[p][l : l + 1, :], (8, 128)) for l in range(8)]
        y = rows[p]
        for j in range(7):
            col = jnp.zeros((8, 128), jnp.float32)
            for i in range(j + 1, 8):
                col = jnp.where(sub == i, n[i][j], col)
            y = y + col * rowb[j]
        d = inv[0]
        for i in range(1, 8):
            d = jnp.where(sub == i, inv[i], d)
        done.append(y * jnp.sqrt(d))
        if p < 7:
            w = y * d
            z = w
            for j in range(1, 8):
                col = jnp.zeros((8, 128), jnp.float32)
                for i in range(j):
                    col = jnp.where(sub == i, n[j][i], col)
                z = z + col * jnp.broadcast_to(w[j : j + 1, :], (8, 128))
            zb = [jnp.broadcast_to(z[l : l + 1, :], (8, 128)) for l in range(8)]
            for q in range(p + 1, 8):
                a = later[q][0] * zb[0]
                b = later[q][1] * zb[1]
                for l in range(2, 8, 2):
                    a = a + later[q][l] * zb[l]
                    b = b + later[q][l + 1] * zb[l + 1]
                rows[q] = rows[q] - (a + b)
    return jnp.concatenate(done, axis=0)


def factor_into(block, work, pad):
    size = TILE
    eye = (lax.broadcasted_iota(jnp.int32, (size, size), 0) == lax.broadcasted_iota(jnp.int32, (size, size), 1))
    work[:, :size] = block
    work[:, size:] = jnp.where(eye, 1.0, 0.0)
    sub = lax.broadcasted_iota(jnp.int32, (8, 128), 0)
    lane = lax.broadcasted_iota(jnp.int32, (STEP, 128), 1)
    row = lax.broadcasted_iota(jnp.int32, (STEP, 128), 0)
    for o in range(size // STEP):
        half = o % 2
        first = o * STEP
        tile = work[first : first + STEP, (o // 2) * 128 : (o // 2) * 128 + 128]
        own = (lane // STEP) == half
        ident = jnp.where(lane - STEP * (1 - half) == row, 1.0, 0.0)
        both = small_block(jnp.where(own, tile, ident), half * STEP, sub)
        x = jnp.where(own, 0.0, both)
        top = (1 - half) * STEP
        pad[top : top + STEP, :] = work[first : first + STEP, :]
        pad[STEP - top : 2 * STEP - top, :] = jnp.zeros((STEP, 2 * size), jnp.float32)
        upper = product(x, pad[...], NN)
        work[first : first + STEP, :] = upper
        if o < size // STEP - 1:
            rest = first + STEP
            work[rest:, :] = work[rest:, :] - product(upper[:, rest:size], upper, TN)


def lower_of(work):
    size = TILE
    r = lax.broadcasted_iota(jnp.int32, (size, size), 0)
    c = lax.broadcasted_iota(jnp.int32, (size, size), 1)
    return jnp.where(r >= c, work[:, :size].T, 0.0)

def work_space():
    return [pltpu.VMEM((TILE, 2 * TILE), F32), pltpu.VMEM((2 * STEP, 2 * TILE), F32)]


def square(count=1):
    return jax.ShapeDtypeStruct((TILE, count * TILE), F32)


def factor_kernel(block_ref, lower_ref, inverse_ref, work, pad):
    factor_into(block_ref[...], work, pad)
    lower_ref[...] = lower_of(work)
    inverse_ref[...] = work[:, TILE:]


def factor(block):
    return pl.pallas_call(
        factor_kernel,
        out_shape=[square(), square()],
        in_specs=[VMEM],
        out_specs=[VMEM, VMEM],
        scratch_shapes=work_space(),
        cost_estimate=cost(13, 3 * TILE * TILE * 4),
    )(block)


def child_kernel(
    scal, pattern, own, following, lead, lower, inverse, front, panel_ref, weight_ref, pivots_ref
):
    me, miss, core = scal[0], scal[1], scal[2]
    inv = inverse[...]
    below = product(jnp.where(pattern[me, 0] > 0, own[:, :TILE], 0.0), inv, NT)
    panel_ref[...] = jnp.where(me == 0, lower[...], below)
    row = jnp.where(me < miss, jnp.minimum(me + 1, 15), me)

    def block(b):
        kept = (pattern[row, b] > 0) & (me != miss)
        at = slice(b * TILE, (b + 1) * TILE)
        return jnp.where(kept, jnp.where(me < miss, following[:, at], own[:, at]), 0.0)

    weight = product(product(block(0), inv, NT), inv, NN)
    weight_ref[...] = weight
    pair = jnp.concatenate(
        [
            jnp.where(pattern[1, 0] > 0, lead[:TILE], 0.0),
            jnp.where(pattern[2, 0] > 0, lead[TILE:], 0.0),
        ],
        axis=0,
    )
    change = product(weight, pair, NT)
    update_1 = block(1) - change[:, :TILE]
    update_2 = block(2) - change[:, TILE:]
    pivot_0 = jnp.where(miss > 0, update_1, 0.0)
    pivot_1 = jnp.where(miss > 1, update_2, jnp.where(miss < 1, update_1, 0.0))
    pivots_ref[:, :TILE] = pivot_0 + jnp.where(core == 0, front[...], 0.0)
    pivots_ref[:, TILE:] = pivot_1 + jnp.where(core == 1, front[...], 0.0)


def child_rows(scal, pattern, raw, following, lead, lower, inverse, front):
    def wide(count):
        return pl.BlockSpec((TILE, count * TILE), lambda i: (0, 0))

    two = pl.BlockSpec((2 * TILE, TILE), lambda i: (0, 0))
    return pl.pallas_call(
        child_kernel,
        out_shape=[square(), square(), square(2)],
        grid=(1,),
        in_specs=[SMEM, SMEM, wide(3), wide(3), two, wide(1), wide(1), wide(1)],
        out_specs=[wide(1), wide(1), wide(2)],
        cost_estimate=cost(6, 14 * TILE * TILE * 4),
    )(scal, pattern, raw, following, lead, lower, inverse, front)


def spread_kernel(scal, pattern, weight, *refs):
    (own_a, next_a, col_a, own_b, next_b, col_b, front, base_ref, theirs_ref) = refs
    me, miss, core = scal[0], scal[1], scal[2]
    step = pl.program_id(0) + 1
    row = jnp.where(me < miss, jnp.minimum(me + 1, 15), me)

    def update(c, own, following, column):
        source = jnp.minimum(jnp.where(c < miss, c + 1, c), 15)
        kept = (pattern[row, source] > 0) & (me != miss)
        value = jnp.where(kept, jnp.where(me < miss, following[...], own[...]), 0.0)
        rows = jnp.where(pattern[source, 0] > 0, column[...], 0.0)
        value = value - product(weight[...], rows, NT)
        return jnp.where(c == miss, 0.0, value)

    theirs_ref[...] = update(2 * step + 1 - core, own_b, next_b, col_b)
    base_ref[...] = front[...] + update(2 * step + core, own_a, next_a, col_a)


def child_spread(scal, pattern, weight, raw, following, column, front):
    def source(step, scal, other):
        c = 2 * (step + 1) + jnp.where(other, 1 - scal[2], scal[2])
        return jnp.minimum(jnp.where(c < scal[1], c + 1, c), 15)

    def own_block(other):
        return pl.BlockSpec(
            (TILE, TILE),
            lambda i, s, p: (0, jnp.where(s[0] > s[1], source(i, s, other), 0)),
        )

    def next_block(other):
        return pl.BlockSpec(
            (TILE, TILE),
            lambda i, s, p: (0, jnp.where(s[0] < s[1], source(i, s, other) - 2, 0)),
        )

    def row_block(other):
        def place(i, s, p):
            block = source(i, s, other)
            return (lax.rem(block // 2 - s[0] // 2 + 8, 8) * 2 + lax.rem(block, 2), 0)

        return pl.BlockSpec((TILE, TILE), place)

    out = pl.BlockSpec((TILE, TILE), lambda i, s, p: (0, i))
    return pl.pallas_call(
        spread_kernel,
        out_shape=[square(7), square(7)],
        grid_spec=pltpu.PrefetchScalarGridSpec(
            num_scalar_prefetch=2,
            grid=(7,),
            in_specs=[pl.BlockSpec((TILE, TILE), lambda i, s, p: (0, 0))]
            + [own_block(False), next_block(False), row_block(False)]
            + [own_block(True), next_block(True), row_block(True)]
            + [pl.BlockSpec((TILE, TILE), lambda i, s, p: (0, i + 1))],
            out_specs=[out, out],
        ),
        cost_estimate=cost(8, 40 * TILE * TILE * 4),
    )(scal, pattern, weight, raw, following, column, raw, following, column, front)


def pivot_kernel(scal, held, other, pivots, panel_ref, weights_ref, work, pad):
    me, core = scal[0], scal[2]
    row_0 = jnp.where(core == 0, held[:, :TILE], other[:, :TILE])
    row_1 = jnp.where(core == 0, other[...], held[...])
    factor_into(row_0, work, pad)
    lower_0, inverse_0 = lower_of(work), work[:, TILE:]
    below_10 = product(row_1[:, :TILE], inverse_0, NT)
    below_0 = product(pivots[:, :TILE], inverse_0, NT)
    panel_ref[...] = jnp.where(me == 0, lower_0, below_0)
    rest = pivots[:, TILE:] - product(below_0, below_10, NT)
    weight_0 = product(below_0, inverse_0, NN)
    weight_10 = product(below_10, inverse_0, NN)
    factor_into(row_1[:, TILE:] - product(below_10, below_10, NT), work, pad)
    inverse_1 = work[:, TILE:]
    below_1 = product(rest, inverse_1, NT)
    weight_1 = product(below_1, inverse_1, NN)
    weights_ref[:, TILE:] = weight_1
    weights_ref[:, :TILE] = weight_0 - product(weight_1, weight_10, NN)
    lower_1 = lower_of(work)

    @pl.when(core == 1)
    def _():
        panel_ref[...] = jnp.where(me == 0, 0.0, jnp.where(me == 1, lower_1, below_1))


def parent_pivots(scal, held, other, pivots):
    return pl.pallas_call(
        pivot_kernel,
        out_shape=[square(), square(2)],
        in_specs=[SMEM, VMEM, VMEM, VMEM],
        out_specs=[VMEM, VMEM],
        scratch_shapes=work_space(),
        cost_estimate=cost(36, 9 * TILE * TILE * 4),
    )(scal, held, other, pivots)


def schur_kernel(scal, panel, base, theirs, weights, rows, out_ref):
    step = pl.program_id(0)

    @pl.when(step == 0)
    def _():
        out_ref[...] = panel[...]

    @pl.when(step > 0)
    def _():
        value = base[...] + theirs[...] - product(weights[...], rows[...], NT)
        out_ref[...] = jnp.where(scal[0] < 2, 0.0, value)


def schur(scal, panel, base, theirs, weights, rows):
    before = pl.BlockSpec((TILE, TILE), lambda i, s: (0, jnp.maximum(i - 1, 0)))
    return pl.pallas_call(
        schur_kernel,
        out_shape=square(8),
        grid_spec=pltpu.PrefetchScalarGridSpec(
            num_scalar_prefetch=1,
            grid=(8,),
            in_specs=[
                pl.BlockSpec((TILE, TILE), lambda i, s: (0, 0)),
                before,
                before,
                pl.BlockSpec((TILE, 2 * TILE), lambda i, s: (0, 0)),
                pl.BlockSpec((TILE, 2 * TILE), lambda i, s: (lax.rem(i - s[0] // 2 + 8, 8), 0)),
            ],
            out_specs=pl.BlockSpec((TILE, TILE), lambda i, s: (0, i)),
        ),
        cost_estimate=cost(8, 40 * TILE * TILE * 4),
    )(scal, panel, base, theirs, weights, rows)


def tied(value, *after):
    return lax.optimization_barrier((value, *after))[0]


def send_grp(block, pairs):
    return lax.ppermute(block, "grp", pairs)


def swap_core(block):
    return lax.ppermute(block, "sub", [(i, i ^ 1) for i in range(16)])


def ring_z(block):
    up_pairs = [(i, (i + 2) % 16) for i in range(16)]
    down_pairs = [(i, (i - 2) % 16) for i in range(16)]
    below, above = [block], [block]
    for _ in range(3):
        below.append(send_grp(below[-1], up_pairs))
        above.append(send_grp(above[-1], down_pairs))
    half = block.shape[0] // 2
    far = [send_grp(below[-1][:half], up_pairs), send_grp(above[-1][half:], down_pairs)]
    return jnp.concatenate(above + far + below[:0:-1], axis=0)


def on_device(child_fronts, child_pattern, child_maps, parent_fronts):
    raw = child_fronts[0]
    nblocks = raw.shape[1] // TILE
    me = lax.axis_index("grp")
    core = lax.axis_index("sub") % 2
    z, x = me // 2, me % 2
    pattern = child_pattern[0]
    front = parent_fronts[0]
    miss = jnp.sum((child_maps[0] == jnp.arange(nblocks - 1)).astype(jnp.int32))
    scal = jnp.stack([me, miss, core]).astype(jnp.int32)
    first = raw[:, :TILE]

    partner = send_grp(first, [(i, i ^ 1) for i in range(16)])
    pair = jnp.concatenate(
        [jnp.where(x == 0, first, partner), jnp.where(x == 0, partner, first)], axis=0
    )
    head_next = send_grp(tied(raw[:, : 3 * TILE], partner), [((i + 1) % 16, i) for i in range(16)])
    column = ring_z(pair)

    def rows_of(whole, rows, place):
        return lax.dynamic_slice_in_dim(whole, lax.rem(place - z + 8, 8) * rows, TILE, 0)

    corner = rows_of(column, 2 * TILE, 0)
    shifted = jnp.concatenate([column[TILE:], column[:TILE]], axis=0)
    lead = jnp.concatenate([rows_of(shifted, 2 * TILE, 0), rows_of(column, 2 * TILE, 1)], axis=0)

    rest = raw[:, 2 * TILE :]
    middle = rest.shape[1] // 2
    even = send_grp(tied(rest, head_next), [(2 * p + 1, 2 * p) for p in range(8)])
    rest = tied(rest, column)
    odd_a = send_grp(rest[:, :middle], [((2 * p + 2) % 16, 2 * p + 1) for p in range(8)])
    odd_b = send_grp(rest[:, middle:], [((2 * p + 2) % 16, 2 * p) for p in range(8)])
    odd_b = send_grp(odd_b, [(2 * p, 2 * p + 1) for p in range(8)])
    tail_next = jnp.where(x == 0, even, jnp.concatenate([odd_a, odd_b], axis=1))

    lower, inverse = factor(corner)
    child_panels, weight, pivots = child_rows(
        scal, pattern, raw, head_next, lead, lower, inverse, front
    )
    pivots = pivots + swap_core(pivots)

    pairs = []
    for sub in range(16):
        for place in range(8):
            source, target = place * 2 + sub % 2, place * 2 + 1 - sub % 2
            pairs.append((sub * 16 + source, sub * 16 + target))
    across = lax.ppermute(pivots, ("sub", "grp"), pairs)
    rows = ring_z(jnp.where(x == core, pivots, across))
    held = rows_of(rows, TILE, 0)
    other = swap_core(held)

    base, theirs = child_spread(scal, pattern, weight, raw, tail_next, column, front)
    received = swap_core(theirs)
    panel, weights = parent_pivots(scal, held, other, pivots)
    result = schur(scal, panel, base, received, weights, rows)
    return (child_panels[None], result[None])


def solution(mesh):
    in_specs = (P("sub", "grp", None), P("sub", None, None), P("sub", None), P("sub", "grp", None))
    out_specs = (P("sub", "grp", None), P("sub", "grp", None))
    return jax.shard_map(
        on_device, mesh=mesh, in_specs=in_specs, out_specs=out_specs, check_vma=False
    )
```

```python
import jax
import jax.numpy as jnp
from jax import lax
from jax.experimental import pallas as pl
from jax.experimental.pallas import tpu as pltpu
from jax.sharding import PartitionSpec as P

TILE = 256
STEP = 64
NN, NT, TN = ((1,), (0,)), ((1,), (1,)), ((0,), (0,))
F32 = jnp.float32
SMEM = pl.BlockSpec(memory_space=pltpu.SMEM)
VMEM = pl.BlockSpec(memory_space=pltpu.VMEM)


def product(a, b, dims):
    return lax.dot_general(
        a, b, (dims, ((), ())), precision=lax.Precision.HIGHEST, preferred_element_type=F32
    )


def cost(us, moved):
    return pl.CostEstimate(flops=int(us * 1e9), bytes_accessed=moved, transcendentals=0)


def small_block(tile, base, sub):
    rows = [tile[8 * q : 8 * q + 8, :] for q in range(8)]
    done = []
    for p in range(8):
        lanes = [base + 8 * p + l for l in range(8)]
        def column(q, l):
            return jnp.broadcast_to(rows[q][:, lanes[l] : lanes[l] + 1], (8, 128))
        own = [column(p, l) for l in range(8)]
        s = [[None] * 8 for _ in range(8)]
        for i in range(8):
            for l in range(i + 1):
                s[i][l] = jnp.broadcast_to(own[l][i : i + 1, :], (8, 128))
        later = {q: [column(q, l) for l in range(8)] for q in range(p + 1, 8)}
        m = [[None] * 8 for _ in range(8)]
        inv = []
        for j in range(8):
            r = 1.0 / s[j][j]
            inv.append(r)
            for i in range(j + 1, 8):
                m[i][j] = s[i][j] * r
            for i in range(j + 1, 8):
                for k in range(j + 1, i + 1):
                    s[i][k] = s[i][k] - m[i][j] * s[k][j]
        n = [[None] * 8 for _ in range(8)]
        for j in range(8):
            for i in range(j + 1, 8):
                total = m[i][j]
                for k in range(j + 1, i):
                    total = total + m[i][k] * n[k][j]
                n[i][j] = -total
        rowb = [jnp.broadcast_to(rows[p][l : l + 1, :], (8, 128)) for l in range(8)]
        y = rows[p]
        for j in range(7):
            col = jnp.zeros((8, 128), jnp.float32)
            for i in range(j + 1, 8):
                col = jnp.where(sub == i, n[i][j], col)
            y = y + col * rowb[j]
        d = inv[0]
        for i in range(1, 8):
            d = jnp.where(sub == i, inv[i], d)
        done.append(y * jnp.sqrt(d))
        if p < 7:
            w = y * d
            z = w
            for j in range(1, 8):
                col = jnp.zeros((8, 128), jnp.float32)
                for i in range(j):
                    col = jnp.where(sub == i, n[j][i], col)
                z = z + col * jnp.broadcast_to(w[j : j + 1, :], (8, 128))
            zb = [jnp.broadcast_to(z[l : l + 1, :], (8, 128)) for l in range(8)]
            for q in range(p + 1, 8):
                a = later[q][0] * zb[0]
                b = later[q][1] * zb[1]
                for l in range(2, 8, 2):
                    a = a + later[q][l] * zb[l]
                    b = b + later[q][l + 1] * zb[l + 1]
                rows[q] = rows[q] - (a + b)
    return jnp.concatenate(done, axis=0)


def factor_into(block, work, pad):
    size = TILE
    eye = (lax.broadcasted_iota(jnp.int32, (size, size), 0) == lax.broadcasted_iota(jnp.int32, (size, size), 1))
    work[:, :size] = block
    work[:, size:] = jnp.where(eye, 1.0, 0.0)
    sub = lax.broadcasted_iota(jnp.int32, (8, 128), 0)
    lane = lax.broadcasted_iota(jnp.int32, (STEP, 128), 1)
    row = lax.broadcasted_iota(jnp.int32, (STEP, 128), 0)
    for o in range(size // STEP):
        half = o % 2
        first = o * STEP
        tile = work[first : first + STEP, (o // 2) * 128 : (o // 2) * 128 + 128]
        own = (lane // STEP) == half
        ident = jnp.where(lane - STEP * (1 - half) == row, 1.0, 0.0)
        both = small_block(jnp.where(own, tile, ident), half * STEP, sub)
        x = jnp.where(own, 0.0, both)
        top = (1 - half) * STEP
        pad[top : top + STEP, :] = work[first : first + STEP, :]
        pad[STEP - top : 2 * STEP - top, :] = jnp.zeros((STEP, 2 * size), jnp.float32)
        upper = product(x, pad[...], NN)
        work[first : first + STEP, :] = upper
        if o < size // STEP - 1:
            rest = first + STEP
            work[rest:, :] = work[rest:, :] - product(upper[:, rest:size], upper, TN)


def lower_of(work):
    size = TILE
    r = lax.broadcasted_iota(jnp.int32, (size, size), 0)
    c = lax.broadcasted_iota(jnp.int32, (size, size), 1)
    return jnp.where(r >= c, work[:, :size].T, 0.0)

def work_space():
    return [pltpu.VMEM((TILE, 2 * TILE), F32), pltpu.VMEM((2 * STEP, 2 * TILE), F32)]


def square(count=1):
    return jax.ShapeDtypeStruct((TILE, count * TILE), F32)


def factor_kernel(block_ref, lower_ref, inverse_ref, work, pad):
    factor_into(block_ref[...], work, pad)
    lower_ref[...] = lower_of(work)
    inverse_ref[...] = work[:, TILE:]


def factor(block):
    return pl.pallas_call(
        factor_kernel,
        out_shape=[square(), square()],
        in_specs=[VMEM],
        out_specs=[VMEM, VMEM],
        scratch_shapes=work_space(),
        cost_estimate=cost(13, 3 * TILE * TILE * 4),
    )(block)


def child_kernel(
    scal, pattern, own, following, lead, lower, inverse, front, panel_ref, weight_ref, pivots_ref
):
    me, miss, core = scal[0], scal[1], scal[2]
    inv = inverse[...]
    below = product(jnp.where(pattern[me, 0] > 0, own[:, :TILE], 0.0), inv, NT)
    panel_ref[...] = jnp.where(me == 0, lower[...], below)
    row = jnp.where(me < miss, jnp.minimum(me + 1, 15), me)

    def block(b):
        kept = (pattern[row, b] > 0) & (me != miss)
        at = slice(b * TILE, (b + 1) * TILE)
        return jnp.where(kept, jnp.where(me < miss, following[:, at], own[:, at]), 0.0)

    weight = product(product(block(0), inv, NT), inv, NN)
    weight_ref[...] = weight
    pair = jnp.concatenate(
        [
            jnp.where(pattern[1, 0] > 0, lead[:TILE], 0.0),
            jnp.where(pattern[2, 0] > 0, lead[TILE:], 0.0),
        ],
        axis=0,
    )
    change = product(weight, pair, NT)
    update_1 = block(1) - change[:, :TILE]
    update_2 = block(2) - change[:, TILE:]
    pivot_0 = jnp.where(miss > 0, update_1, 0.0)
    pivot_1 = jnp.where(miss > 1, update_2, jnp.where(miss < 1, update_1, 0.0))
    pivots_ref[:, :TILE] = pivot_0 + jnp.where(core == 0, front[...], 0.0)
    pivots_ref[:, TILE:] = pivot_1 + jnp.where(core == 1, front[...], 0.0)


def child_rows(scal, pattern, raw, following, lead, lower, inverse, front):
    def wide(count):
        return pl.BlockSpec((TILE, count * TILE), lambda i: (0, 0))

    two = pl.BlockSpec((2 * TILE, TILE), lambda i: (0, 0))
    return pl.pallas_call(
        child_kernel,
        out_shape=[square(), square(), square(2)],
        grid=(1,),
        in_specs=[SMEM, SMEM, wide(3), wide(3), two, wide(1), wide(1), wide(1)],
        out_specs=[wide(1), wide(1), wide(2)],
        cost_estimate=cost(6, 14 * TILE * TILE * 4),
    )(scal, pattern, raw, following, lead, lower, inverse, front)


def spread_kernel(scal, pattern, weight, *refs):
    sources, (front, base_ref, theirs_ref) = (refs[:6], refs[6:12]), refs[12:]
    me, miss, core = scal[0], scal[1], scal[2]
    step = pl.program_id(0) + 1
    row = jnp.where(me < miss, jnp.minimum(me + 1, 15), me)

    def update(c, own, even_a, even_b, odd_a, odd_b, column):
        source = jnp.minimum(jnp.where(c < miss, c + 1, c), 15)
        kept = (pattern[row, source] > 0) & (me != miss)
        even = jnp.where(source < 9, even_a[...], even_b[...])
        odd = jnp.where(source < 9, odd_a[...], odd_b[...])
        following = jnp.where(lax.rem(me, 2) == 0, even, odd)
        value = jnp.where(kept, jnp.where(me < miss, following, own[...]), 0.0)
        rows = jnp.where(pattern[source, 0] > 0, column[...], 0.0)
        value = value - product(weight[...], rows, NT)
        return jnp.where(c == miss, 0.0, value)

    theirs_ref[...] = update(2 * step + 1 - core, *sources[1])
    base_ref[...] = front[...] + update(2 * step + core, *sources[0])


def child_spread(scal, pattern, weight, raw, even_a, even_b, odd_a, odd_b, column, front):
    def specs(other):
        def source(step, scal):
            c = 2 * (step + 1) + jnp.where(other, 1 - scal[2], scal[2])
            return jnp.minimum(jnp.where(c < scal[1], c + 1, c), 15)

        def strip(wanted, first, last):
            def place(i, s, p):
                block = jnp.clip(source(i, s), first, last) - first
                return (0, jnp.where(wanted(s), block, 0))

            return pl.BlockSpec((TILE, TILE), place)

        def row_place(i, s, p):
            block = source(i, s)
            return (lax.rem(block // 2 - s[0] // 2 + 8, 8) * 2 + lax.rem(block, 2), 0)

        return [
            strip(lambda s: s[0] > s[1], 0, 15),
            strip(lambda s: (s[0] < s[1]) & (lax.rem(s[0], 2) == 0), 2, 8),
            strip(lambda s: (s[0] < s[1]) & (lax.rem(s[0], 2) == 0), 9, 15),
            strip(lambda s: (s[0] < s[1]) & (lax.rem(s[0], 2) == 1), 2, 8),
            strip(lambda s: (s[0] < s[1]) & (lax.rem(s[0], 2) == 1), 9, 15),
            pl.BlockSpec((TILE, TILE), row_place),
        ]

    out = pl.BlockSpec((TILE, TILE), lambda i, s, p: (0, i))
    return pl.pallas_call(
        spread_kernel,
        out_shape=[square(7), square(7)],
        grid_spec=pltpu.PrefetchScalarGridSpec(
            num_scalar_prefetch=2,
            grid=(7,),
            in_specs=[pl.BlockSpec((TILE, TILE), lambda i, s, p: (0, 0))]
            + specs(False)
            + specs(True)
            + [pl.BlockSpec((TILE, TILE), lambda i, s, p: (0, i + 1))],
            out_specs=[out, out],
        ),
        cost_estimate=cost(8, 40 * TILE * TILE * 4),
        compiler_params=pltpu.CompilerParams(vmem_limit_bytes=24 * 1024 * 1024),
    )(scal, pattern, weight, *[raw, even_a, even_b, odd_a, odd_b, column] * 2, front)


def pivot_kernel(scal, held, other, pivots, panel_ref, weights_ref, work, pad):
    me, core = scal[0], scal[2]
    row_0 = jnp.where(core == 0, held[:, :TILE], other[:, :TILE])
    row_1 = jnp.where(core == 0, other[...], held[...])
    factor_into(row_0, work, pad)
    lower_0, inverse_0 = lower_of(work), work[:, TILE:]
    below_10 = product(row_1[:, :TILE], inverse_0, NT)
    below_0 = product(pivots[:, :TILE], inverse_0, NT)
    panel_ref[...] = jnp.where(me == 0, lower_0, below_0)
    rest = pivots[:, TILE:] - product(below_0, below_10, NT)
    weight_0 = product(below_0, inverse_0, NN)
    weight_10 = product(below_10, inverse_0, NN)
    factor_into(row_1[:, TILE:] - product(below_10, below_10, NT), work, pad)
    inverse_1 = work[:, TILE:]
    below_1 = product(rest, inverse_1, NT)
    weight_1 = product(below_1, inverse_1, NN)
    weights_ref[:, TILE:] = weight_1
    weights_ref[:, :TILE] = weight_0 - product(weight_1, weight_10, NN)
    lower_1 = lower_of(work)

    @pl.when(core == 1)
    def _():
        panel_ref[...] = jnp.where(me == 0, 0.0, jnp.where(me == 1, lower_1, below_1))


def parent_pivots(scal, held, other, pivots):
    return pl.pallas_call(
        pivot_kernel,
        out_shape=[square(), square(2)],
        in_specs=[SMEM, VMEM, VMEM, VMEM],
        out_specs=[VMEM, VMEM],
        scratch_shapes=work_space(),
        compiler_params=pltpu.CompilerParams(vmem_limit_bytes=16 * 1024 * 1024),
        cost_estimate=cost(27, 9 * TILE * TILE * 4),
    )(scal, held, other, pivots)


def schur_kernel(scal, panel, base, theirs, weights, *refs):
    rows, out_ref = refs[:-1], refs[-1]
    step = pl.program_id(0)
    place = lax.rem(step + scal[0] // 2, 8)

    @pl.when(place == 0)
    def _():
        out_ref[...] = panel[...]

    for k in range(8):

        @pl.when((place > 0) & (step == k))
        def _():
            value = base[...] + theirs[...] - product(weights[...], rows[k][...], NT)
            out_ref[...] = jnp.where(scal[0] < 2, 0.0, value)


def schur(scal, panel, base, theirs, weights, rows):
    def whole(count):
        return pl.BlockSpec((TILE, count * TILE), lambda i, s: (0, 0))

    def block(i, s):
        return lax.rem(i + s[0] // 2, 8)

    before = pl.BlockSpec((TILE, TILE), lambda i, s: (0, jnp.maximum(block(i, s) - 1, 0)))
    return pl.pallas_call(
        schur_kernel,
        out_shape=square(8),
        grid_spec=pltpu.PrefetchScalarGridSpec(
            num_scalar_prefetch=1,
            grid=(8,),
            in_specs=[whole(1), before, before, whole(2)] + [whole(2)] * 8,
            out_specs=pl.BlockSpec((TILE, TILE), lambda i, s: (0, block(i, s))),
        ),
        compiler_params=pltpu.CompilerParams(vmem_limit_bytes=20 * 1024 * 1024),
        cost_estimate=cost(8, 40 * TILE * TILE * 4),
    )(scal, panel, base, theirs, weights, *rows)


def tied(value, *after):
    return lax.optimization_barrier((value, *after))[0]


def send_grp(block, pairs):
    return lax.ppermute(block, "grp", pairs)


def swap_core(block):
    return lax.ppermute(block, "sub", [(i, i ^ 1) for i in range(16)])


def up(block):
    return send_grp(block, [(i, (i + 2) % 16) for i in range(16)])


def down(block):
    return send_grp(block, [(i, (i - 2) % 16) for i in range(16)])


def ring_near(block):
    below, above = [block], [block]
    for _ in range(3):
        below.append(up(below[-1]))
        above.append(down(above[-1]))
    return above, below


def ring_far(near):
    above, below = near
    half = above[0].shape[0] // 2
    far = jnp.concatenate([up(below[3][:half]), down(above[3][half:])], axis=0)
    return above + [far] + below[:0:-1]


def on_device(child_fronts, child_pattern, child_maps, parent_fronts):
    raw = child_fronts[0]
    nblocks = raw.shape[1] // TILE
    me = lax.axis_index("grp")
    core = lax.axis_index("sub") % 2
    z, x = me // 2, me % 2
    pattern = child_pattern[0]
    front = parent_fronts[0]
    miss = jnp.sum((child_maps[0] == jnp.arange(nblocks - 1)).astype(jnp.int32))
    scal = jnp.stack([me, miss, core]).astype(jnp.int32)
    first = raw[:, :TILE]

    partner = send_grp(first, [(i, i ^ 1) for i in range(16)])
    pair = jnp.concatenate(
        [jnp.where(x == 0, first, partner), jnp.where(x == 0, partner, first)], axis=0
    )
    head_next = send_grp(tied(raw[:, : 3 * TILE], partner), [((i + 1) % 16, i) for i in range(16)])

    middle = (nblocks // 2 + 1) * TILE
    left, right = raw[:, 2 * TILE : middle], raw[:, middle:]
    left, right, _ = lax.optimization_barrier((left, right, partner))
    along = [(2 * p + 1, 2 * p) for p in range(8)]
    against = [(2 * p, 2 * p + 1) for p in range(8)]
    even_a = send_grp(left, along)
    odd_a = send_grp(left, against)
    pieces = ring_far(ring_near(pair))

    def pick(pieces, place, rows):
        slot = lax.rem(place - z + 8, 8)
        value = pieces[0][rows]
        for k in range(1, 8):
            value = jnp.where(slot == k, pieces[k][rows], value)
        return value

    corner = pick(pieces, 0, slice(0, TILE))
    lead = jnp.concatenate(
        [pick(pieces, 0, slice(TILE, 2 * TILE)), pick(pieces, 1, slice(0, TILE))], axis=0
    )
    corner, odd_a, odd_b = lax.optimization_barrier((corner, odd_a, right))
    odd_a = send_grp(odd_a, [((2 * p + 3) % 16, 2 * p + 1) for p in range(8)])
    odd_b = send_grp(odd_b, [((2 * p + 2) % 16, 2 * p) for p in range(8)])

    lower, inverse = factor(corner)
    lead, even_a = lax.optimization_barrier((lead, even_a))
    child_panels, weight, pivots = child_rows(
        scal, pattern, raw, head_next, lead, lower, inverse, front
    )
    pivots = pivots + swap_core(pivots)

    pairs = []
    for sub in range(16):
        for place in range(8):
            source, target = place * 2 + sub % 2, place * 2 + 1 - sub % 2
            pairs.append((sub * 16 + source, sub * 16 + target))
    across = lax.ppermute(pivots, ("sub", "grp"), pairs)
    mine = jnp.where(x == core, pivots, across)
    mine, odd_a, odd_b, right = lax.optimization_barrier((mine, odd_a, odd_b, right))
    even_b = send_grp(right, along)
    odd_b = send_grp(odd_b, against)
    near = ring_near(mine)
    base, theirs = child_spread(
        scal, pattern, weight, raw, even_a, even_b, odd_a, odd_b, jnp.concatenate(pieces, axis=0), front
    )
    near, base, theirs = lax.optimization_barrier((near, base, theirs))
    rows = ring_far(near)
    received = swap_core(theirs)
    held = pick(rows, 0, slice(None))
    other = swap_core(held)
    panel, weights = parent_pivots(scal, held, other, pivots)
    result = schur(scal, panel, base, received, weights, rows)
    return (child_panels[None], result[None])


def solution(mesh):
    in_specs = (P("sub", "grp", None), P("sub", None, None), P("sub", None), P("sub", "grp", None))
    out_specs = (P("sub", "grp", None), P("sub", "grp", None))
    return jax.shard_map(
        on_device, mesh=mesh, in_specs=in_specs, out_specs=out_specs, check_vma=False
    )
```
